32 devices in a mesh: groups: 2 (over x), expert: 8 (over z, y), cuts: 2 (over core).
Axes of the slice: x: 2, y: 2, z: 4, core: 2. Of those that a mesh axis runs over, the one named last changes fastest.
Arguments:
- tokens: bfloat16 [64, 2, 6144], P(('groups', 'expert', 'cuts')), parts along dimension 0, may hold values from -6 to 6
- routes: int32 [64, 2, 2], P(('groups', 'expert', 'cuts')), parts along dimension 0, may hold values from 0 to 7, all different within a row
- gates: float32 [64, 2, 2], P(('groups', 'expert', 'cuts')), parts along dimension 0, may hold values from 0.1 to 0.9
- ranking: int32 [16], P('groups'), parts along dimension 0, may hold values from 0 to 7, each once
- counts: int32 [2, 32], P(None, ('groups', 'expert', 'cuts')), parts along dimension 1, may hold values from 1 to 2, 24 in all within a row
- w_gate: bfloat16 [2, 6144, 8192], P(None, None, ('expert', 'cuts')), may hold values from -0.078125 to 0.078125
- w_up: bfloat16 [2, 6144, 8192], P(None, None, ('expert', 'cuts')), may hold values from -0.078125 to 0.078125
- w_down: bfloat16 [2, 8192, 6144], P(None, ('expert', 'cuts')), may hold values from -0.0625 to 0.0625
Outputs:
- expert_out: bfloat16 [64, 2, 6144], P(('groups', 'expert', 'cuts')), parts along dimension 0
The draws below stay inside these ranges and needn't reach their ends.
There are 2 independent parts, one for each index of `groups`. The reference program is written for one: setup_inputs(seed, part) draws one part's arguments, and reference() takes and returns one part's arrays. A program takes and returns all parts, laid end to end along the dimension named above; an argument that names none is the same for every part. Nothing has to cross between parts.
All inputs are finite; a program needn't handle non-finite values. No bound on the sum of `counts` on one device may be relied on, other than what follows from the above.
Results may differ from the reference program's by a relative error of at most 0.0067.
Values may be sent and summed in bfloat16 or wider, within the bound.
A program may use at most 128 MiB of HBM per device.

```python
import math
import jax
import jax.numpy as jnp
import numpy as np
from jax import lax

D = 6144
FF = 8192
EXPERTS = 8
TOP = 2
HOT = 2
STEPS = 2
TOK_DEV = 2
DEVS = 16
TOKENS = 32


def block_scale(stream_key, shape, shards, least, high):
    def one(axis_at, blocks):
        draws = jax.random.uniform(jax.random.fold_in(jax.random.fold_in(stream_key, 6), axis_at), (blocks,), jnp.float32, least / len(shards), high / len(shards))
        return jnp.repeat(jnp.exp(draws), shape[axis_at] // blocks).reshape((-1,) + (1,) * (len(shape) - axis_at - 1))

    loudness = one(*shards[0])
    for cut in shards[1:]:
        loudness = loudness * one(*cut)
    return loudness


def different_ones(rng, rows, number_of, top, lift):
    sequence = jax.random.permutation(jax.random.fold_in(rng, 1), number_of)
    pull = sequence
    for power in range(3):
        pull = pull * pull // number_of
    pull = pull * lift // number_of
    chance = jax.random.randint(jax.random.fold_in(rng, 2), (rows, number_of), 0, 4096) + pull
    holders = jax.random.permutation(jax.random.fold_in(rng, 3), rows)[jnp.arange(number_of) % rows]
    chance = jnp.where(jnp.arange(rows)[:, None] == holders[None, :], 1 << 14, chance)
    priority = chance * number_of + jnp.arange(number_of)
    return lax.top_k(priority.astype(jnp.int32), top)[1].astype(jnp.int32)


def split_up(number_of, total, bound, skew):
    weights = [(1 << 20) // math.isqrt(standing ** skew) + 1 for standing in range(2, number_of + 1)]
    surplus, holding = total - bound - (number_of - 1), [1] * (number_of - 1)
    while surplus > 0:
        movable = [i for i in range(number_of - 1) if holding[i] < bound]
        mass, budget = sum([weights[i] for i in movable]), surplus
        for i in movable:
            more = min(bound - holding[i], max(1, budget * weights[i] // mass), surplus)
            holding[i] = holding[i] + more
            surplus = surplus - more
    return np.array([bound] + holding)


def ragged_sizes(own_key, amount, total, most, slope):
    if amount == 2:
        one = jax.random.randint(own_key, (), max(1, total - most), min(most, total - 1) + 1)
        return jnp.stack([one, total - one])
    lengths = jnp.asarray(split_up(amount, total, most, slope), jnp.int32)
    twos = (amount - 1) // 2
    donor, sink = lengths[1:1 + 2 * twos:2], lengths[2:2 + 2 * twos:2]
    room = jnp.minimum(donor - 1, most - sink)
    moved = jax.random.randint(jax.random.fold_in(own_key, 1), (twos,), 0, 1 << 20) % (room + 1)
    lengths = lengths.at[1:1 + 2 * twos:2].set(donor - moved).at[2:2 + 2 * twos:2].set(sink + moved)
    return lengths[jax.random.permutation(jax.random.fold_in(own_key, 2), amount)]


def bell_draw(stream_key, extent, scale, limit, cuts=(), kind=jnp.bfloat16):
    result = scale * jax.random.normal(stream_key, extent, jnp.float32)
    if cuts:
        result = result * block_scale(stream_key, extent, cuts, -0.22, 0.18)
    return jnp.clip(result, -limit, limit).astype(kind)


def setup_inputs(seed: int = 0, part: int = 0) -> dict:
    key_of = jax.random.split(jax.random.key(seed), 9)
    own_keys = jax.random.split(jax.random.fold_in(key_of[8], part), 9)
    return {
        "tokens": bell_draw(own_keys[0], (TOKENS, STEPS, D), 1.0, 6.0, ((0, 16),)),
        "routes": different_ones(own_keys[1], TOKENS * STEPS, EXPERTS, TOP, 4096).reshape((TOKENS, STEPS, TOP)),
        "gates": jnp.clip(0.1 + 0.79999997 * jax.random.uniform(own_keys[2], (TOKENS, STEPS, TOP), jnp.float32) ** block_scale(own_keys[2], (TOKENS, STEPS, TOP), ((0, 16),), -0.2, 0.2), 0.1, 0.9),
        "ranking": jax.random.permutation(own_keys[3], EXPERTS).astype(jnp.int32),
        "counts": jax.vmap(lambda own: ragged_sizes(own, DEVS, DEVS * TOK_DEV * 3 // 4, TOK_DEV, 2))(jax.random.split(own_keys[4], STEPS)).reshape((STEPS, DEVS)).astype(jnp.int32),
        "w_gate": bell_draw(key_of[5], (HOT, D, FF), D ** -0.5, 0.078125, ((2, 16),)),
        "w_up": bell_draw(key_of[6], (HOT, D, FF), D ** -0.5, 0.078125, ((2, 16),)),
        "w_down": bell_draw(key_of[7], (HOT, FF, D), FF ** -0.5, 0.0625, ((1, 16),)),
    }


def reference(tokens, routes, gates, ranking, counts, w_gate, w_up, w_down):
    hot = ranking[:HOT]
    match = (routes[:, :, :, None] == hot[None, None, None, :]).astype(jnp.float32)
    weight = jnp.sum(gates[:, :, :, None] * match, axis=2)
    rows = jnp.arange(TOKENS, dtype=jnp.int32)
    owner = rows // TOK_DEV
    slot = rows % TOK_DEV
    live = (slot[:, None] < jnp.transpose(counts[:, owner])).astype(jnp.float32)
    weight = (weight * live[:, :, None]).astype(jnp.bfloat16)
    inputs = tokens.astype(jnp.float32)
    total = jnp.zeros((TOKENS, STEPS, D), jnp.float32)
    for which in range(HOT):
        gate = jnp.einsum("nsd,df->nsf", inputs, w_gate[which].astype(jnp.float32))
        upper = jnp.einsum("nsd,df->nsf", inputs, w_up[which].astype(jnp.float32))
        scale = weight[:, :, which:which + 1].astype(jnp.float32)
        hidden = (jax.nn.silu(gate) * upper * scale).astype(jnp.bfloat16)
        total = total + jnp.einsum("nsf,fd->nsd", hidden.astype(jnp.float32), w_down[which].astype(jnp.float32))
    return total.astype(jnp.bfloat16)
```

```python
import functools

import jax
import jax.numpy as jnp
from jax import lax
from jax.experimental import pallas as pl
from jax.experimental.pallas import tpu as pltpu
from jax.sharding import PartitionSpec as P

HOT = 2
LANES = 128
K_PARTS = 4
COL_PARTS = 6
MESH = pl.DeviceIdType.MESH


def kernel(
    planes, tokens, routes, gates, ranking, counts, w_gate, w_up, w_down, out,
    gathered, rows_f32, rows, gate_w, up_w, down_w, g_acc, u_acc, hidden,
    send_a, recv_a, send_b, recv_b, send_c, recv_c, total,
    token_sem, gate_sems, up_sems, down_sems,
    gz_send, gz_recv, gy_send, gy_recv, gc_send, gc_recv,
    a_send, a_recv, b_send, b_recv, c_send, c_recv,
):
    own_rows, steps, width = tokens.shape
    block = own_rows * steps
    part = planes * block
    depth = width // K_PARTS
    cols = width // COL_PARTS
    group = lax.axis_index("groups")
    expert = lax.axis_index("expert")
    c = lax.axis_index("cuts")
    z = expert // 2
    y = expert % 2

    def device(zz, yy, cc):
        return (group, zz * 2 + yy, cc)

    def slot(zz, yy, cc):
        return pl.ds(((zz * 2 + yy) * 2 + cc) * own_rows, own_rows)

    def plane(dz):
        return lax.rem(z + dz, planes)

    mine = slot(z, y, c)
    token_copy = pltpu.make_async_copy(
        tokens, gathered.at[mine, :, pl.ds(0, width)], token_sem
    )
    token_copy.start()
    gate_copies, up_copies, down_copies = [], [], []
    for h in range(HOT):
        for k in range(K_PARTS):
            at = pl.ds(k * depth, depth)
            i = h * K_PARTS + k
            gate_copies.append(
                pltpu.make_async_copy(w_gate.at[h, at, :], gate_w.at[h, at, :], gate_sems.at[i])
            )
            up_copies.append(
                pltpu.make_async_copy(w_up.at[h, at, :], up_w.at[h, at, :], up_sems.at[i])
            )
            gate_copies[-1].start()
            up_copies[-1].start()
    for j in range(COL_PARTS):
        at = pl.ds(j * cols, cols)
        down_copies.append(
            pltpu.make_async_copy(w_down.at[:, :, at], down_w.at[j], down_sems.at[j])
        )
        down_copies[-1].start()

    barrier = pltpu.get_barrier_semaphore()
    for dz in range(1, planes):
        pl.semaphore_signal(barrier, inc=1, device_id=device(plane(dz), y, c), device_id_type=MESH)
    pl.semaphore_signal(barrier, inc=1, device_id=device(z, 1 - y, c), device_id_type=MESH)
    pl.semaphore_signal(barrier, inc=1, device_id=device(z, y, 1 - c), device_id_type=MESH)

    lane = lax.broadcasted_iota(jnp.int32, (1, LANES), 1)
    for r in range(own_rows):
        lines = []
        for s in range(steps):
            line = jnp.zeros((1, LANES), jnp.float32)
            for h in range(HOT):
                value = jnp.float32(0)
                for k in range(routes.shape[2]):
                    value = value + jnp.where(routes[r, s, k] == ranking[h], gates[r, s, k], 0.0)
                value = jnp.where(r < counts[s, 0], value, 0.0)
                line = jnp.where(lane == h, value, line)
            lines.append(line)
        own = ((z * 2 + y) * 2 + c) * own_rows + r
        gathered[own, :, pl.ds(width, LANES)] = jnp.concatenate(lines, axis=0).astype(jnp.bfloat16)
    token_copy.wait()
    pl.semaphore_wait(barrier, planes + 1)

    def remote(src, dst, send, recv, target):
        return pltpu.make_async_remote_copy(
            src_ref=src, dst_ref=dst, send_sem=send, recv_sem=recv,
            device_id=target, device_id_type=MESH,
        )

    def share(where, send, recv, target):
        return remote(gathered.at[where], gathered.at[where], send, recv, target)

    to_y, to_c = device(z, 1 - y, c), device(z, y, 1 - c)
    z_copies = [
        share(mine, gz_send.at[dz], gz_recv.at[dz], device(plane(dz), y, c))
        for dz in range(1, planes)
    ]
    y_copies = [
        share(slot(plane(planes - dz), y, c), gy_send.at[dz], gy_recv.at[dz], to_y)
        for dz in range(planes)
    ]
    c_copies = [
        [
            share(
                slot(plane(planes - dz), yy, c),
                gc_send.at[i * planes + dz], gc_recv.at[i * planes + dz], to_c,
            )
            for dz in range(planes)
        ]
        for i, yy in enumerate((y, 1 - y))
    ]
    for copy in z_copies:
        copy.start()
    y_copies[0].start()
    c_copies[0][0].start()
    for dz in range(1, planes):
        z_copies[dz - 1].wait_recv()
        y_copies[dz].start()
        c_copies[0][dz].start()
    for dz in range(planes):
        y_copies[dz].wait_recv()
        c_copies[1][dz].start()
    for i in range(2):
        for copy in c_copies[i]:
            copy.wait_recv()

    for dc in range(2):
        for dy in range(2):
            for dz in range(planes):
                cc = 1 - c if dc == 0 else c
                yy = 1 - y if dy == 0 else y
                first = ((plane(dz) * 2 + yy) * 2 + cc) * own_rows
                base = ((dc * 2 + dy) * planes + dz) * block
                for r in range(own_rows):
                    rows_f32[base + r * steps:base + (r + 1) * steps, :] = gathered[
                        first + r
                    ].astype(jnp.float32)
    rows[...] = rows_f32[:, :width].astype(jnp.bfloat16)

    for h in range(HOT):
        for k in range(K_PARTS):
            i = h * K_PARTS + k
            at = slice(k * depth, (k + 1) * depth)
            gate_copies[i].wait()
            g = jnp.dot(rows[:, at], gate_w[h, at, :], preferred_element_type=jnp.float32)
            up_copies[i].wait()
            u = jnp.dot(rows[:, at], up_w[h, at, :], preferred_element_type=jnp.float32)
            if k == 0:
                g_acc[...] = g
                u_acc[...] = u
            else:
                g_acc[...] += g
                u_acc[...] += u
        g = g_acc[...]
        weight = rows_f32[:, width + h:width + h + 1]
        hidden[h] = (g / (1.0 + jnp.exp(-g)) * u_acc[...] * weight).astype(jnp.bfloat16)

    a_copies = [
        remote(send_a.at[j], recv_a.at[j], a_send.at[j], a_recv.at[j], to_c)
        for j in range(COL_PARTS)
    ]
    b_copies = [
        remote(send_b.at[j], recv_b.at[j], b_send.at[j], b_recv.at[j], to_y)
        for j in range(COL_PARTS)
    ]
    d_copies = [
        [
            remote(
                send_c.at[j, dz], recv_c.at[j, dz],
                c_send.at[j * planes + dz], c_recv.at[j * planes + dz],
                device(plane(dz), y, c),
            )
            for dz in range(1, planes)
        ]
        for j in range(COL_PARTS)
    ]

    def down(j):
        down_copies[j].wait()
        p = jnp.dot(hidden[0], down_w[j, 0], preferred_element_type=jnp.float32)
        p = p + jnp.dot(hidden[1], down_w[j, 1], preferred_element_type=jnp.float32)
        send_a[j] = p[:2 * part].astype(jnp.bfloat16)
        a_copies[j].start()
        total[j] = p[2 * part:]

    def after_a(j):
        a_copies[j].wait_recv()
        send_b[j] = (total[j, :part] + recv_a[j, :part].astype(jnp.float32)).astype(jnp.bfloat16)
        b_copies[j].start()
        total[j, part:] += recv_a[j, part:].astype(jnp.float32)

    def after_b(j):
        b_copies[j].wait_recv()
        total[j, part:] += recv_b[j].astype(jnp.float32)
        for dz in range(1, planes):
            base = part + dz * block
            send_c[j, dz] = total[j, base:base + block].astype(jnp.bfloat16)
            d_copies[j][dz - 1].start()

    def after_c(j):
        result = total[j, part:part + block]
        for dz in range(1, planes):
            d_copies[j][dz - 1].wait_recv()
            result = result + recv_c[j, dz].astype(jnp.float32)
        for r in range(own_rows):
            out[r, :, j * cols:(j + 1) * cols] = result[r * steps:(r + 1) * steps].astype(jnp.bfloat16)

    for j in range(COL_PARTS + 3):
        if j < COL_PARTS:
            down(j)
        if 0 <= j - 1 < COL_PARTS:
            after_a(j - 1)
        if 0 <= j - 2 < COL_PARTS:
            after_b(j - 2)
    for j in range(COL_PARTS):
        after_c(j)

    for copy in z_copies + y_copies + c_copies[0] + c_copies[1] + a_copies + b_copies:
        copy.wait_send()
    for copies in d_copies:
        for copy in copies:
            copy.wait_send()


def on_device(devices, tokens, routes, gates, ranking, counts, w_gate, w_up, w_down):
    own_rows, steps, width = tokens.shape
    planes = devices // 4
    block = own_rows * steps
    part = planes * block
    units = w_gate.shape[2]
    cols = width // COL_PARTS
    bf16, f32 = jnp.bfloat16, jnp.float32
    dma = pltpu.SemaphoreType.DMA
    in_vmem = pl.BlockSpec(memory_space=pltpu.VMEM)
    in_smem = pl.BlockSpec(memory_space=pltpu.SMEM)
    anywhere = pl.BlockSpec(memory_space=pl.ANY)
    return pl.pallas_call(
        functools.partial(kernel, planes),
        out_shape=jax.ShapeDtypeStruct(tokens.shape, bf16),
        in_specs=[anywhere] + [in_smem] * 4 + [anywhere] * 3,
        out_specs=in_vmem,
        scratch_shapes=[
            pltpu.VMEM((devices * own_rows, steps, width + LANES), bf16),
            pltpu.VMEM((4 * part, width + LANES), f32),
            pltpu.VMEM((4 * part, width), bf16),
            pltpu.VMEM((HOT, width, units), bf16),
            pltpu.VMEM((HOT, width, units), bf16),
            pltpu.VMEM((COL_PARTS, HOT, units, cols), bf16),
            pltpu.VMEM((4 * part, units), f32),
            pltpu.VMEM((4 * part, units), f32),
            pltpu.VMEM((HOT, 4 * part, units), bf16),
            pltpu.VMEM((COL_PARTS, 2 * part, cols), bf16),
            pltpu.VMEM((COL_PARTS, 2 * part, cols), bf16),
            pltpu.VMEM((COL_PARTS, part, cols), bf16),
            pltpu.VMEM((COL_PARTS, part, cols), bf16),
            pltpu.VMEM((COL_PARTS, planes, block, cols), bf16),
            pltpu.VMEM((COL_PARTS, planes, block, cols), bf16),
            pltpu.VMEM((COL_PARTS, 2 * part, cols), f32),
            dma,
            dma((HOT * K_PARTS,)),
            dma((HOT * K_PARTS,)),
            dma((COL_PARTS,)),
            dma((planes,)), dma((planes,)),
            dma((planes,)), dma((planes,)),
            dma((2 * planes,)), dma((2 * planes,)),
            dma((COL_PARTS,)), dma((COL_PARTS,)),
            dma((COL_PARTS,)), dma((COL_PARTS,)),
            dma((COL_PARTS * planes,)), dma((COL_PARTS * planes,)),
        ],
        compiler_params=pltpu.CompilerParams(
            collective_id=0, has_side_effects=True, vmem_limit_bytes=60 << 20
        ),
    )(tokens, routes, gates, ranking, counts, w_gate, w_up, w_down)


def solution(mesh):
    rows = ("groups", "expert", "cuts")
    units = ("expert", "cuts")
    in_specs = (
        P(rows, None, None),
        P(rows, None, None),
        P(rows, None, None),
        P("groups"),
        P(None, rows),
        P(None, None, units),
        P(None, None, units),
        P(None, units, None),
    )
    devices = mesh.shape["expert"] * mesh.shape["cuts"]
    return jax.shard_map(
        functools.partial(on_device, devices), mesh=mesh, in_specs=in_specs,
        out_specs=P(rows, None, None), check_vma=False,
    )
```

```python
import functools

import jax
import jax.numpy as jnp
from jax import lax
from jax.experimental import pallas as pl
from jax.experimental.pallas import tpu as pltpu
from jax.sharding import PartitionSpec as P

HOT = 2
LANES = 128
K_PARTS = 4
COL_PARTS = 6
FIRST = 6
STEP = 3
LAG = 3
MESH = pl.DeviceIdType.MESH


def kernel(
    planes, tokens, routes_hbm, gates_hbm, ranking_hbm, counts_hbm, w_gate, w_up, w_down, out,
    routes, gates, ranking, counts, own_tokens, own_block, small_sems,
    gathered, rows_f32, rows, gate_w, up_w, down_w, g_acc, u_acc, hidden,
    send_a, recv_a, send_b, recv_b, send_c, recv_c, total,
    token_sem, gate_sems, up_sems, down_sems,
    gz_send, gz_recv, gy_send, gy_recv, gc_send, gc_recv,
    a_send, a_recv, b_send, b_recv, c_send, c_recv,
):
    own_rows, steps, width = tokens.shape
    block = own_rows * steps
    part = planes * block
    depth = width // K_PARTS
    cols = width // COL_PARTS
    group = lax.axis_index("groups")
    expert = lax.axis_index("expert")
    c = lax.axis_index("cuts")
    z = expert // 2
    y = expert % 2

    def device(zz, yy, cc):
        return (group, zz * 2 + yy, cc)

    def slot(zz, yy, cc):
        return (zz * 2 + yy) * 2 + cc

    def plane(dz):
        return lax.rem(z + dz, planes)

    to_y, to_c = device(z, 1 - y, c), device(z, y, 1 - c)
    barrier = pltpu.get_barrier_semaphore()
    for target in [device(plane(dz), y, c) for dz in range(1, planes)] + [to_y, to_c]:
        pl.semaphore_signal(barrier, inc=1, device_id=target, device_id_type=MESH)

    small_copies = [
        pltpu.make_async_copy(src, dst, small_sems.at[i])
        for i, (src, dst) in enumerate((
            (routes_hbm, routes), (gates_hbm, gates), (ranking_hbm, ranking), (counts_hbm, counts)
        ))
    ]
    token_copy = pltpu.make_async_copy(tokens, own_tokens, token_sem)
    token_copy.start()
    for copy in small_copies:
        copy.start()

    gate_copies, up_copies, down_copies, waiting = [], [], [], []
    for h in range(HOT):
        for k in range(K_PARTS):
            at = pl.ds(k * depth, depth)
            i = h * K_PARTS + k
            gate_copies.append(
                pltpu.make_async_copy(w_gate.at[h, at, :], gate_w.at[h, at, :], gate_sems.at[i])
            )
            up_copies.append(
                pltpu.make_async_copy(w_up.at[h, at, :], up_w.at[h, at, :], up_sems.at[i])
            )
            waiting += [gate_copies[-1], up_copies[-1]]
    for j in range(COL_PARTS):
        at = pl.ds(j * cols, cols)
        down_copies.append(
            pltpu.make_async_copy(w_down.at[:, :, at], down_w.at[j], down_sems.at[j])
        )
    waiting += down_copies

    def stream(count):
        for copy in waiting[:count]:
            copy.start()
        del waiting[:count]

    stream(FIRST)
    for copy in small_copies:
        copy.wait()

    mine = slot(z, y, c)
    lane = lax.broadcasted_iota(jnp.int32, (1, LANES), 1)
    for r in range(own_rows):
        for s in range(steps):
            line = jnp.zeros((1, LANES), jnp.float32)
            for h in range(HOT):
                value = jnp.float32(0)
                for k in range(routes.shape[2]):
                    value = value + jnp.where(routes[r, s, k] == ranking[h], gates[r, s, k], 0.0)
                value = jnp.where(r < counts[s], value, 0.0)
                line = jnp.where(lane == h, value, line)
            own_block[r * steps + s:r * steps + s + 1, width:] = line
    token_copy.wait()
    for r in range(own_rows):
        own_block[r * steps:(r + 1) * steps, :width] = own_tokens[r].astype(jnp.float32)
    gathered[mine] = own_block[...].astype(jnp.bfloat16)
    pl.semaphore_wait(barrier, planes + 1)

    def remote(src, dst, send, recv, target):
        return pltpu.make_async_remote_copy(
            src_ref=src, dst_ref=dst, send_sem=send, recv_sem=recv,
            device_id=target, device_id_type=MESH,
        )

    def share(where, send, recv, target):
        return remote(gathered.at[where], gathered.at[where], send, recv, target)

    z_copies = [
        share(mine, gz_send.at[dz], gz_recv.at[dz], device(plane(dz), y, c))
        for dz in range(1, planes)
    ]
    y_copies = [
        share(slot(plane(planes - dz), y, c), gy_send.at[dz], gy_recv.at[dz], to_y)
        for dz in range(planes)
    ]
    c_copies = [
        [
            share(
                slot(plane(planes - dz), yy, c),
                gc_send.at[i * planes + dz], gc_recv.at[i * planes + dz], to_c,
            )
            for dz in range(planes)
        ]
        for i, yy in enumerate((y, 1 - y))
    ]

    def keep(dc, dy, back):
        dz = (planes - back) % planes
        base = ((dc * 2 + dy) * planes + dz) * block
        source = slot(plane(dz), y if dy else 1 - y, c if dc else 1 - c)
        rows_f32[base:base + block, :] = gathered[source].astype(jnp.float32)

    for copy in z_copies:
        copy.start()
    y_copies[0].start()
    c_copies[0][0].start()
    stream(STEP)
    keep(1, 1, 0)
    for back in range(1, planes + 1):
        if back < planes:
            z_copies[back - 1].wait_recv()
            y_copies[back].start()
            c_copies[0][back].start()
            stream(STEP)
            keep(1, 1, back)
        y_copies[back - 1].wait_recv()
        c_copies[1][back - 1].start()
        stream(STEP)
        keep(1, 0, back - 1)
    stream(len(waiting))
    for back in range(planes):
        c_copies[0][back].wait_recv()
        keep(0, 1, back)
    for back in range(planes):
        c_copies[1][back].wait_recv()
        keep(0, 0, back)
    rows[...] = rows_f32[:, :width].astype(jnp.bfloat16)

    for h in range(HOT):
        for k in range(K_PARTS):
            i = h * K_PARTS + k
            at = slice(k * depth, (k + 1) * depth)
            gate_copies[i].wait()
            g = jnp.dot(rows[:, at], gate_w[h, at, :], preferred_element_type=jnp.float32)
            up_copies[i].wait()
            u = jnp.dot(rows[:, at], up_w[h, at, :], preferred_element_type=jnp.float32)
            if k == 0:
                g_acc[...] = g
                u_acc[...] = u
            else:
                g_acc[...] += g
                u_acc[...] += u
        g = g_acc[...]
        weight = rows_f32[:, width + h:width + h + 1]
        hidden[h] = (g / (1.0 + jnp.exp(-g)) * u_acc[...] * weight).astype(jnp.bfloat16)

    a_copies = [
        remote(send_a.at[j], recv_a.at[j], a_send.at[j], a_recv.at[j], to_c)
        for j in range(COL_PARTS)
    ]
    b_copies = [
        remote(send_b.at[j], recv_b.at[j], b_send.at[j], b_recv.at[j], to_y)
        for j in range(COL_PARTS)
    ]
    d_copies = [
        [
            remote(
                send_c.at[j, dz], recv_c.at[j, dz],
                c_send.at[j * planes + dz], c_recv.at[j * planes + dz],
                device(plane(dz), y, c),
            )
            for dz in range(1, planes)
        ]
        for j in range(COL_PARTS)
    ]

    def down(j):
        down_copies[j].wait()
        p = jnp.dot(hidden[0], down_w[j, 0], preferred_element_type=jnp.float32)
        p = p + jnp.dot(hidden[1], down_w[j, 1], preferred_element_type=jnp.float32)
        send_a[j] = p[:2 * part].astype(jnp.bfloat16)
        a_copies[j].start()
        total[j] = p[2 * part:]

    def after_a(j):
        a_copies[j].wait_recv()
        send_b[j] = (total[j, :part] + recv_a[j, :part].astype(jnp.float32)).astype(jnp.bfloat16)
        b_copies[j].start()
        total[j, part:] += recv_a[j, part:].astype(jnp.float32)

    def after_b(j):
        b_copies[j].wait_recv()
        total[j, part:] += recv_b[j].astype(jnp.float32)
        for dz in range(1, planes):
            base = part + dz * block
            send_c[j, dz] = total[j, base:base + block].astype(jnp.bfloat16)
            d_copies[j][dz - 1].start()

    def after_c(j):
        result = total[j, part:part + block]
        for dz in range(1, planes):
            d_copies[j][dz - 1].wait_recv()
            result = result + recv_c[j, dz].astype(jnp.float32)
        for r in range(own_rows):
            out[r, :, j * cols:(j + 1) * cols] = result[r * steps:(r + 1) * steps].astype(jnp.bfloat16)

    for j in range(COL_PARTS + 2 * LAG):
        if j < COL_PARTS:
            down(j)
        if 0 <= j - LAG < COL_PARTS:
            after_a(j - LAG)
        if 0 <= j - 2 * LAG < COL_PARTS:
            after_b(j - 2 * LAG)
    for j in range(COL_PARTS):
        after_c(j)

    for copy in z_copies + y_copies + c_copies[0] + c_copies[1] + a_copies + b_copies:
        copy.wait_send()
    for copies in d_copies:
        for copy in copies:
            copy.wait_send()


def on_device(devices, tokens, routes, gates, ranking, counts, w_gate, w_up, w_down):
    counts = counts.reshape(-1)
    own_rows, steps, width = tokens.shape
    planes = devices // 4
    block = own_rows * steps
    part = planes * block
    units = w_gate.shape[2]
    cols = width // COL_PARTS
    bf16, f32 = jnp.bfloat16, jnp.float32
    dma = pltpu.SemaphoreType.DMA
    in_vmem = pl.BlockSpec(memory_space=pltpu.VMEM)
    smem = pltpu.SMEM
    anywhere = pl.BlockSpec(memory_space=pl.ANY)
    return pl.pallas_call(
        functools.partial(kernel, planes),
        out_shape=jax.ShapeDtypeStruct(tokens.shape, bf16),
        in_specs=[anywhere] * 8,
        out_specs=in_vmem,
        scratch_shapes=[
            smem(routes.shape, routes.dtype),
            smem(gates.shape, gates.dtype),
            smem(ranking.shape, ranking.dtype),
            smem(counts.shape, counts.dtype),
            pltpu.VMEM(tokens.shape, bf16),
            pltpu.VMEM((block, width + LANES), f32),
            dma((4,)),
            pltpu.VMEM((devices, block, width + LANES), bf16),
            pltpu.VMEM((4 * part, width + LANES), f32),
            pltpu.VMEM((4 * part, width), bf16),
            pltpu.VMEM((HOT, width, units), bf16),
            pltpu.VMEM((HOT, width, units), bf16),
            pltpu.VMEM((COL_PARTS, HOT, units, cols), bf16),
            pltpu.VMEM((4 * part, units), f32),
            pltpu.VMEM((4 * part, units), f32),
            pltpu.VMEM((HOT, 4 * part, units), bf16),
            pltpu.VMEM((COL_PARTS, 2 * part, cols), bf16),
            pltpu.VMEM((COL_PARTS, 2 * part, cols), bf16),
            pltpu.VMEM((COL_PARTS, part, cols), bf16),
            pltpu.VMEM((COL_PARTS, part, cols), bf16),
            pltpu.VMEM((COL_PARTS, planes, block, cols), bf16),
            pltpu.VMEM((COL_PARTS, planes, block, cols), bf16),
            pltpu.VMEM((COL_PARTS, 2 * part, cols), f32),
            dma,
            dma((HOT * K_PARTS,)),
            dma((HOT * K_PARTS,)),
            dma((COL_PARTS,)),
            dma((planes,)), dma((planes,)),
            dma((planes,)), dma((planes,)),
            dma((2 * planes,)), dma((2 * planes,)),
            dma((COL_PARTS,)), dma((COL_PARTS,)),
            dma((COL_PARTS,)), dma((COL_PARTS,)),
            dma((COL_PARTS * planes,)), dma((COL_PARTS * planes,)),
        ],
        compiler_params=pltpu.CompilerParams(
            collective_id=0, has_side_effects=True, vmem_limit_bytes=60 << 20
        ),
    )(tokens, routes, gates, ranking, counts, w_gate, w_up, w_down)


def solution(mesh):
    rows = ("groups", "expert", "cuts")
    units = ("expert", "cuts")
    in_specs = (
        P(rows, None, None),
        P(rows, None, None),
        P(rows, None, None),
        P("groups"),
        P(None, rows),
        P(None, None, units),
        P(None, None, units),
        P(None, units, None),
    )
    devices = mesh.shape["expert"] * mesh.shape["cuts"]
    return jax.shard_map(
        functools.partial(on_device, devices), mesh=mesh, in_specs=in_specs,
        out_specs=P(rows, None, None), check_vma=False,
    )
```

```python
import functools

import jax
import jax.numpy as jnp
from jax import lax
from jax.experimental import pallas as pl
from jax.experimental.pallas import tpu as pltpu
from jax.sharding import PartitionSpec as P

HOT = 2
LANES = 128
K_PARTS = 2
COL_PARTS = 4
FIRST = 2
STEP = 2
LAG = 2
MESH = pl.DeviceIdType.MESH


def kernel(
    planes, tokens, routes_hbm, gates_hbm, ranking_hbm, counts_hbm, w_gate, w_up, w_down, out,
    routes, gates, ranking, counts, own_tokens, own_block, small_sems,
    gathered, rows_f32, rows, gate_w, up_w, down_w, g_acc, u_acc, hidden,
    send_a, recv_a, send_b, recv_b, send_c, recv_c, total,
    token_sem, gate_sems, up_sems, down_sems,
    gz_send, gz_recv, gy_send, gy_recv, gc_send, gc_recv,
    a_send, a_recv, b_send, b_recv, c_send, c_recv,
):
    own_rows, steps, width = tokens.shape
    block = own_rows * steps
    part = planes * block
    depth = width // K_PARTS
    cols = width // COL_PARTS
    group = lax.axis_index("groups")
    expert = lax.axis_index("expert")
    c = lax.axis_index("cuts")
    z = expert // 2
    y = expert % 2

    def device(zz, yy, cc):
        return (group, zz * 2 + yy, cc)

    def slot(zz, yy, cc):
        return (zz * 2 + yy) * 2 + cc

    def plane(dz):
        return lax.rem(z + dz, planes)

    to_y, to_c = device(z, 1 - y, c), device(z, y, 1 - c)
    barrier = pltpu.get_barrier_semaphore()
    for target in [device(plane(dz), y, c) for dz in range(1, planes)] + [to_y, to_c]:
        pl.semaphore_signal(barrier, inc=1, device_id=target, device_id_type=MESH)

    small_copies = [
        pltpu.make_async_copy(src, dst, small_sems.at[i])
        for i, (src, dst) in enumerate((
            (routes_hbm, routes), (gates_hbm, gates), (ranking_hbm, ranking), (counts_hbm, counts)
        ))
    ]
    token_copy = pltpu.make_async_copy(tokens, own_tokens, token_sem)
    token_copy.start()
    for copy in small_copies:
        copy.start()

    gate_copies, up_copies, down_copies, waiting = [], [], [], []
    for h in range(HOT):
        for k in range(K_PARTS):
            at = pl.ds(k * depth, depth)
            i = h * K_PARTS + k
            gate_copies.append(
                pltpu.make_async_copy(w_gate.at[h, at, :], gate_w.at[h, at, :], gate_sems.at[i])
            )
            up_copies.append(
                pltpu.make_async_copy(w_up.at[h, at, :], up_w.at[h, at, :], up_sems.at[i])
            )
            waiting += [gate_copies[-1], up_copies[-1]]
    for j in range(COL_PARTS):
        at = pl.ds(j * cols, cols)
        down_copies.append(
            pltpu.make_async_copy(w_down.at[:, :, at], down_w.at[j], down_sems.at[j])
        )
    waiting += down_copies

    def stream(count):
        for copy in waiting[:count]:
            copy.start()
        del waiting[:count]

    stream(FIRST)
    for copy in small_copies:
        copy.wait()

    mine = slot(z, y, c)
    lane = lax.broadcasted_iota(jnp.int32, (1, LANES), 1)
    for r in range(own_rows):
        for s in range(steps):
            line = jnp.zeros((1, LANES), jnp.float32)
            for h in range(HOT):
                value = jnp.float32(0)
                for k in range(routes.shape[2]):
                    value = value + jnp.where(routes[r, s, k] == ranking[h], gates[r, s, k], 0.0)
                value = jnp.where(r < counts[s], value, 0.0)
                line = jnp.where(lane == h, value, line)
            own_block[r * steps + s:r * steps + s + 1, width:] = line
    token_copy.wait()
    for r in range(own_rows):
        own_block[r * steps:(r + 1) * steps, :width] = own_tokens[r].astype(jnp.float32)
    gathered[mine] = own_block[...].astype(jnp.bfloat16)
    pl.semaphore_wait(barrier, planes + 1)

    def remote(src, dst, send, recv, target):
        return pltpu.make_async_remote_copy(
            src_ref=src, dst_ref=dst, send_sem=send, recv_sem=recv,
            device_id=target, device_id_type=MESH,
        )

    def share(where, send, recv, target):
        return remote(gathered.at[where], gathered.at[where], send, recv, target)

    z_copies = [
        share(mine, gz_send.at[dz], gz_recv.at[dz], device(plane(dz), y, c))
        for dz in range(1, planes)
    ]
    y_copies = [
        share(slot(plane(planes - dz), y, c), gy_send.at[dz], gy_recv.at[dz], to_y)
        for dz in range(planes)
    ]
    c_copies = [
        [
            share(
                slot(plane(planes - dz), yy, c),
                gc_send.at[i * planes + dz], gc_recv.at[i * planes + dz], to_c,
            )
            for dz in range(planes)
        ]
        for i, yy in enumerate((y, 1 - y))
    ]

    def keep(dc, dy, back):
        dz = (planes - back) % planes
        base = ((dc * 2 + dy) * planes + dz) * block
        source = slot(plane(dz), y if dy else 1 - y, c if dc else 1 - c)
        rows_f32[base:base + block, :] = gathered[source].astype(jnp.float32)

    for copy in z_copies:
        copy.start()
    y_copies[0].start()
    c_copies[0][0].start()
    stream(STEP)
    keep(1, 1, 0)
    for back in range(1, planes + 1):
        if back < planes:
            z_copies[back - 1].wait_recv()
            y_copies[back].start()
            c_copies[0][back].start()
            stream(STEP)
            keep(1, 1, back)
        y_copies[back - 1].wait_recv()
        c_copies[1][back - 1].start()
        stream(STEP)
        keep(1, 0, back - 1)
    stream(len(waiting))
    for back in range(planes):
        c_copies[0][back].wait_recv()
        keep(0, 1, back)
    for back in range(planes):
        c_copies[1][back].wait_recv()
        keep(0, 0, back)
    rows[...] = rows_f32[:, :width].astype(jnp.bfloat16)

    for h in range(HOT):
        for k in range(K_PARTS):
            i = h * K_PARTS + k
            at = slice(k * depth, (k + 1) * depth)
            gate_copies[i].wait()
            g = jnp.dot(rows[:, at], gate_w[h, at, :], preferred_element_type=jnp.float32)
            up_copies[i].wait()
            u = jnp.dot(rows[:, at], up_w[h, at, :], preferred_element_type=jnp.float32)
            if k == 0:
                g_acc[...] = g
                u_acc[...] = u
            else:
                g_acc[...] += g
                u_acc[...] += u
        g = g_acc[...]
        weight = rows_f32[:, width + h:width + h + 1]
        hidden[h] = (g / (1.0 + jnp.exp(-g)) * u_acc[...] * weight).astype(jnp.bfloat16)

    a_copies = [
        remote(send_a.at[j], recv_a.at[j], a_send.at[j], a_recv.at[j], to_c)
        for j in range(COL_PARTS)
    ]
    b_copies = [
        remote(send_b.at[j], recv_b.at[j], b_send.at[j], b_recv.at[j], to_y)
        for j in range(COL_PARTS)
    ]
    d_copies = [
        [
            remote(
                send_c.at[j, dz], recv_c.at[j, dz],
                c_send.at[j * planes + dz], c_recv.at[j * planes + dz],
                device(plane(dz), y, c),
            )
            for dz in range(1, planes)
        ]
        for j in range(COL_PARTS)
    ]

    def down(j):
        down_copies[j].wait()
        p = jnp.dot(hidden[0], down_w[j, 0], preferred_element_type=jnp.float32)
        p = p + jnp.dot(hidden[1], down_w[j, 1], preferred_element_type=jnp.float32)
        send_a[j] = p[:2 * part].astype(jnp.bfloat16)
        a_copies[j].start()
        total[j] = p[2 * part:]

    def after_a(j):
        a_copies[j].wait_recv()
        send_b[j] = (total[j, :part] + recv_a[j, :part].astype(jnp.float32)).astype(jnp.bfloat16)
        b_copies[j].start()
        total[j, part:] += recv_a[j, part:].astype(jnp.float32)

    def after_b(j):
        b_copies[j].wait_recv()
        total[j, part:] += recv_b[j].astype(jnp.float32)
        for dz in range(1, planes):
            base = part + dz * block
            send_c[j, dz] = total[j, base:base + block].astype(jnp.bfloat16)
            d_copies[j][dz - 1].start()

    def after_c(j):
        result = total[j, part:part + block]
        for dz in range(1, planes):
            d_copies[j][dz - 1].wait_recv()
            result = result + recv_c[j, dz].astype(jnp.float32)
        for r in range(own_rows):
            out[r, :, j * cols:(j + 1) * cols] = result[r * steps:(r + 1) * steps].astype(jnp.bfloat16)

    for j in range(COL_PARTS + 2 * LAG):
        if j < COL_PARTS:
            down(j)
        if 0 <= j - LAG < COL_PARTS:
            after_a(j - LAG)
        if 0 <= j - 2 * LAG < COL_PARTS:
            after_b(j - 2 * LAG)
    for j in range(COL_PARTS):
        after_c(j)

    for copy in z_copies + y_copies + c_copies[0] + c_copies[1] + a_copies + b_copies:
        copy.wait_send()
    for copies in d_copies:
        for copy in copies:
            copy.wait_send()


def on_device(devices, tokens, routes, gates, ranking, counts, w_gate, w_up, w_down):
    counts = counts.reshape(-1)
    own_rows, steps, width = tokens.shape
    planes = devices // 4
    block = own_rows * steps
    part = planes * block
    units = w_gate.shape[2]
    cols = width // COL_PARTS
    bf16, f32 = jnp.bfloat16, jnp.float32
    dma = pltpu.SemaphoreType.DMA
    in_vmem = pl.BlockSpec(memory_space=pltpu.VMEM)
    smem = pltpu.SMEM
    anywhere = pl.BlockSpec(memory_space=pl.ANY)
    return pl.pallas_call(
        functools.partial(kernel, planes),
        out_shape=jax.ShapeDtypeStruct(tokens.shape, bf16),
        in_specs=[anywhere] * 8,
        out_specs=in_vmem,
        scratch_shapes=[
            smem(routes.shape, routes.dtype),
            smem(gates.shape, gates.dtype),
            smem(ranking.shape, ranking.dtype),
            smem(counts.shape, counts.dtype),
            pltpu.VMEM(tokens.shape, bf16),
            pltpu.VMEM((block, width + LANES), f32),
            dma((4,)),
            pltpu.VMEM((devices, block, width + LANES), bf16),
            pltpu.VMEM((4 * part, width + LANES), f32),
            pltpu.VMEM((4 * part, width), bf16),
            pltpu.VMEM((HOT, width, units), bf16),
            pltpu.VMEM((HOT, width, units), bf16),
            pltpu.VMEM((COL_PARTS, HOT, units, cols), bf16),
            pltpu.VMEM((4 * part, units), f32),
            pltpu.VMEM((4 * part, units), f32),
            pltpu.VMEM((HOT, 4 * part, units), bf16),
            pltpu.VMEM((COL_PARTS, 2 * part, cols), bf16),
            pltpu.VMEM((COL_PARTS, 2 * part, cols), bf16),
            pltpu.VMEM((COL_PARTS, part, cols), bf16),
            pltpu.VMEM((COL_PARTS, part, cols), bf16),
            pltpu.VMEM((COL_PARTS, planes, block, cols), bf16),
            pltpu.VMEM((COL_PARTS, planes, block, cols), bf16),
            pltpu.VMEM((COL_PARTS, 2 * part, cols), f32),
            dma,
            dma((HOT * K_PARTS,)),
            dma((HOT * K_PARTS,)),
            dma((COL_PARTS,)),
            dma((planes,)), dma((planes,)),
            dma((planes,)), dma((planes,)),
            dma((2 * planes,)), dma((2 * planes,)),
            dma((COL_PARTS,)), dma((COL_PARTS,)),
            dma((COL_PARTS,)), dma((COL_PARTS,)),
            dma((COL_PARTS * planes,)), dma((COL_PARTS * planes,)),
        ],
        compiler_params=pltpu.CompilerParams(
            collective_id=0, has_side_effects=True, vmem_limit_bytes=60 << 20
        ),
    )(tokens, routes, gates, ranking, counts, w_gate, w_up, w_down)


def solution(mesh):
    rows = ("groups", "expert", "cuts")
    units = ("expert", "cuts")
    in_specs = (
        P(rows, None, None),
        P(rows, None, None),
        P(rows, None, None),
        P("groups"),
        P(None, rows),
        P(None, None, units),
        P(None, None, units),
        P(None, units, None),
    )
    devices = mesh.shape["expert"] * mesh.shape["cuts"]
    return jax.shard_map(
        functools.partial(on_device, devices), mesh=mesh, in_specs=in_specs,
        out_specs=P(rows, None, None), check_vma=False,
    )
```
